32 devices in a mesh: rep: 4 (over y, x), fsdp: 8 (over z, core).
Axes of the slice: x: 2, y: 2, z: 4, core: 2. Of those that a mesh axis runs over, the one named last changes fastest.
Arguments:
- acts: bfloat16 [1024, 4096], P(('rep', 'fsdp')), may hold values from -6 to 6
- grad_out: bfloat16 [1024, 14336], P(('rep', 'fsdp')), may hold values from -0.375 to 0.375
- momentum: bfloat16 [4, 4096, 14336], P('rep', 'fsdp'), may hold values from -6 to 6
- band: int32 [32], replicated, may hold values from 0 to 975, as said below
Outputs:
- new_momentum: bfloat16 [4, 4096, 14336], P('rep', 'fsdp')
- update: bfloat16 [4096, 14336], P('fsdp')
The draws below stay inside these ranges and needn't reach their ends.
Inputs may be any that keep to these rules, and one draw needn't show every extreme that they name: `band`: 32 distinct positions u * 64 + v with u and v below 16; 0 and 975 are always among them.
All inputs are finite; a program needn't handle non-finite values.
Results may differ from the reference program's by a relative error of at most 0.007.
Values may be sent and summed in bfloat16 or wider, within the bound.
A program may use at most 384 MiB of HBM per device.

```python
import jax
import jax.numpy as jnp
from jax import lax

D = 4096
FF = 14336
BLOCK = 64
BAND = 32
TOK_DEV = 32
TOKENS = 1024
N_REP = 4
N_FSDP = 8


def draw_band(key, part):
    key = jax.random.fold_in(key, 7)
    inner = jax.random.permutation(key, 254)[:BAND - 2].astype(jnp.int32) + 1
    picks = jnp.concatenate([jnp.zeros((1,), jnp.int32), inner, jnp.full((1,), 255, jnp.int32)])
    return (picks // 16 * BLOCK + picks % 16).astype(jnp.int32)


def block_scale(stream_key, shape, shards, least, top_value):
    gain = 1.0
    for dim, blocks in shards:
        heights = jax.random.uniform(jax.random.fold_in(jax.random.fold_in(stream_key, 6), dim), (blocks,), jnp.float32, least / len(shards), top_value / len(shards))
        gain = gain * jnp.repeat(jnp.exp(heights), shape[dim] // blocks).reshape((-1,) + (1,) * (len(shape) - 1 - dim))
    return gain


def bell_draw(stream_key, shape, spread, most, cuts=(), kind=jnp.bfloat16):
    entries = jax.random.normal(stream_key, shape, jnp.float32) * spread
    if len(cuts) > 0:
        entries = block_scale(stream_key, shape, cuts, -0.22, 0.18) * entries
    return jnp.clip(entries, min=-most, max=most).astype(kind)


def setup_inputs(seed: int = 0) -> dict:
    keys = jax.random.split(jax.random.key(seed), 5)
    return {
        "acts": bell_draw(keys[0], (TOKENS, D), 1.0, 6.0, ((0, 32),)),
        "grad_out": bell_draw(keys[1], (TOKENS, FF), (TOK_DEV * N_FSDP) ** -0.5, 0.375, ((0, 32),)),
        "momentum": bell_draw(keys[2], (N_REP, D, FF), 1.0, 6.0, ((0, 4), (1, 8))),
        "band": draw_band(jax.random.fold_in(keys[4], 71), 0),
    }


momentum_decay = 0.999

def band_basis(band):
    freq = jnp.arange(BLOCK, dtype=jnp.float32)[:, None]
    place = jnp.arange(BLOCK, dtype=jnp.float32)[None, :]
    factor = jnp.where(freq == 0.0, jnp.sqrt(1.0 / BLOCK), jnp.sqrt(2.0 / BLOCK))
    table = factor * jnp.cos(jnp.pi * (2.0 * place + 1.0) * freq / (2.0 * BLOCK))
    levels = jnp.arange(BLOCK, dtype=jnp.int32)[None, :]
    pick_u = (band[:, None] // BLOCK == levels).astype(jnp.float32)
    pick_v = (band[:, None] % BLOCK == levels).astype(jnp.float32)
    rows_u = jnp.dot(pick_u, table, precision=lax.Precision.HIGHEST)
    rows_v = jnp.dot(pick_v, table, precision=lax.Precision.HIGHEST)
    return (rows_u[:, :, None] * rows_v[:, None, :]).astype(jnp.bfloat16)

def project(blocks, basis):
    return jnp.einsum('iajb,kab->ijk', blocks, basis, preferred_element_type=jnp.float32)

def expand(coeffs, basis):
    return jnp.einsum('ijk,kab->iajb', coeffs, basis, preferred_element_type=jnp.float32)

def reference(acts, grad_out, momentum, band):
    basis = band_basis(band)
    group = TOK_DEV * N_FSDP

    def one_replica(items):
        inputs, cotangent, state = items
        grad = jnp.dot(inputs.T, cotangent, preferred_element_type=jnp.float32)
        full = momentum_decay * state.astype(jnp.float32) + grad
        blocks = full.astype(jnp.bfloat16).reshape(D // BLOCK, BLOCK, FF // BLOCK, BLOCK)
        coeffs = project(blocks, basis)
        fresh = (full - expand(coeffs.astype(jnp.bfloat16), basis).reshape(D, FF)).astype(jnp.bfloat16)
        return (fresh, coeffs)
    fresh, coeffs = lax.map(one_replica, (acts.reshape(N_REP, group, D), grad_out.reshape(N_REP, group, FF), momentum))
    mean_coeff = (lax.optimization_barrier(jnp.sum(coeffs, axis=0)) / N_REP).astype(jnp.bfloat16)
    update = expand(mean_coeff, basis).reshape(D, FF).astype(jnp.bfloat16)
    return (fresh, update)
```

```python
import functools

import jax
import jax.numpy as jnp
import ml_dtypes
import numpy as np
from jax import lax
from jax.experimental import pallas as pl
from jax.experimental.pallas import tpu as pltpu
from jax.sharding import PartitionSpec as P

BLOCK = 64
LOW = 16
GROUP = 512
LAG = 1

momentum_decay = 0.999
MESH = pl.DeviceIdType.MESH
BF16 = jnp.bfloat16


def dct_low():
    u = np.arange(LOW, dtype=np.float64)[:, None]
    a = np.arange(BLOCK, dtype=np.float64)[None, :]
    scale = np.where(u == 0, np.sqrt(1.0 / BLOCK), np.sqrt(2.0 / BLOCK))
    return scale * np.cos(np.pi * (2 * a + 1) * u / (2 * BLOCK))


def tables(rows):
    low_dct = dct_low()
    all_cols = np.kron(np.eye(GROUP // BLOCK), low_dct)
    all_rows = np.kron(np.eye(rows // BLOCK), low_dct)
    ch, cl = np_split(all_cols)
    rh, rl = np_split(all_rows)
    fold = np.concatenate([ch.T, cl.T], axis=1)
    unfold = np.concatenate([ch, cl], axis=0)
    spread = np.concatenate([rh.T, rl.T], axis=1)
    return fold, unfold, rh, rl, spread


def np_split(table):
    high = table.astype(ml_dtypes.bfloat16)
    low = (table - high.astype(np.float64)).astype(ml_dtypes.bfloat16)
    return high, low


def dot(a, b):
    return jnp.dot(a, b, preferred_element_type=jnp.float32)


def gather_kernel(
    n_rep, n_fsdp, width, chunks,
    band, acts, gout, momentum, fold, rh, rl,
    at_out, g_out, own_out, mean_out,
    acts_all, g_all, at_v, mom, c_all, mask,
    a_recv, a_send, a_local, g_local, g_recv, line_send, left_send, sib_send,
    m_sem, c_recv, c_send, o_sem, t_sem,
):
    rep = lax.axis_index("rep")
    me = lax.axis_index("fsdp")
    core = lax.rem(me, 2)
    pos = me // 2
    places = n_fsdp // 2
    sib = me + 1 - 2 * core
    rows = at_v.shape[0]
    toks = gout.shape[0]
    low_width = width // BLOCK * LOW

    barrier = pltpu.get_barrier_semaphore()
    for d in range(1, n_fsdp):
        pl.semaphore_signal(
            barrier, inc=1, device_id=(rep, lax.rem(me + d, n_fsdp)), device_id_type=MESH
        )
    for d in range(1, n_rep):
        pl.semaphore_signal(
            barrier, inc=1, device_id=(lax.rem(rep + d, n_rep), me), device_id_type=MESH
        )

    def cols(n):
        return pl.ds(pl.multiple_of(n * width, width), width)

    def low_cols(n):
        return pl.ds(pl.multiple_of(n * low_width, low_width), low_width)

    def load_mom(n):
        return pltpu.make_async_copy(
            momentum.at[0, :, cols(n)], mom.at[lax.rem(n, 2)], m_sem.at[lax.rem(n, 2)]
        )

    own_acts = pltpu.make_async_copy(
        acts.at[:, pl.ds(pl.multiple_of(me * rows, rows), rows)], acts_all.at[me], a_local
    )
    own_acts.start()
    own_g = pltpu.make_async_copy(gout, g_all.at[me], g_local)
    own_g.start()
    load_mom(0).start()

    pl.semaphore_wait(barrier, n_fsdp - 1 + n_rep - 1)

    def acts_copy(d):
        peer = lax.rem(me + d, n_fsdp)
        return pltpu.make_async_remote_copy(
            src_ref=acts.at[:, pl.ds(pl.multiple_of(peer * rows, rows), rows)],
            dst_ref=acts_all.at[me],
            send_sem=a_send.at[d],
            recv_sem=a_recv.at[me],
            device_id=(rep, peer),
            device_id_type=MESH,
        )

    def g_copy(src, b, n, send, target):
        return pltpu.make_async_remote_copy(
            src_ref=src,
            dst_ref=g_all.at[b, :, cols(n)],
            send_sem=send,
            recv_sem=g_recv.at[b, n],
            device_id=(rep, target),
            device_id_type=MESH,
        )

    def slot(b, n):
        return g_all.at[b, :, cols(n)]

    def own_right(n):
        return g_copy(gout.at[:, cols(n)], me, n, line_send.at[pos, n], me + 2)

    def own_left(n):
        return g_copy(gout.at[:, cols(n)], me, n, left_send.at[n], me - 2)

    def own_sib(n):
        return g_copy(gout.at[:, cols(n)], me, n, sib_send.at[pos, n], sib)

    def forward(q, n, target):
        b = 2 * q + core
        return g_copy(slot(b, n), b, n, line_send.at[q, n], target)

    def to_sib(q, n):
        b = 2 * q + core
        return g_copy(slot(b, n), b, n, sib_send.at[q, n], sib)

    def wait_block(b, n):
        pltpu.make_async_copy(slot(b, n), slot(b, n), g_recv.at[b, n]).wait()

    def send_own(n):
        @pl.when(pos + 1 < places)
        def _():
            own_right(n).start()

        @pl.when(pos > 0)
        def _():
            own_left(n).start()

        own_sib(n).start()

    def c_copy(d, n):
        peer = lax.rem(rep + d, n_rep)
        return pltpu.make_async_remote_copy(
            src_ref=c_all.at[rep, :, low_cols(n)],
            dst_ref=c_all.at[rep, :, low_cols(n)],
            send_sem=c_send.at[d, n],
            recv_sem=c_recv.at[rep, n],
            device_id=(peer, me),
            device_id_type=MESH,
        )

    for d in range(1, n_fsdp):
        acts_copy(d).start()
    send_own(0)
    send_own(1)

    low_rows = lax.broadcasted_iota(jnp.int32, mask.shape, 0)
    low_lanes = lax.broadcasted_iota(jnp.int32, mask.shape, 1)
    place = lax.rem(low_rows, LOW) * BLOCK + lax.rem(low_lanes, LOW)
    kept = jnp.zeros(mask.shape, jnp.float32)
    for k in range(band.shape[0]):
        kept = jnp.where(place == band[k], 1.0, kept)
    mask[...] = kept

    own_acts.wait()
    own_g.wait()
    for d in range(1, n_fsdp):
        b = lax.rem(me + d, n_fsdp)
        pltpu.make_async_copy(acts_all.at[b], acts_all.at[b], a_recv.at[b]).wait()
    for b in range(n_fsdp):
        at_v[:, b * toks:(b + 1) * toks] = (
            acts_all[b].astype(jnp.float32).T.astype(BF16)
        )
    at_copy = pltpu.make_async_copy(at_v, at_out, t_sem)
    at_copy.start()

    def out_copy(n):
        return pltpu.make_async_copy(g_all.at[:, :, cols(n)], g_out.at[:, :, cols(n)], o_sem.at[n])

    def step(t, _):
        @pl.when(t + 2 < chunks)
        def _():
            send_own(t + 2)

        for h in range(1, places):
            n = t + 1 - h

            @pl.when((n >= 0) & (n < chunks) & (pos >= h))
            def _():
                q = pos - h
                wait_block(2 * q + core, n)

                @pl.when(pos + 1 < places)
                def _():
                    forward(q, n, me + 2).start()

                to_sib(q, n).start()

            @pl.when((n >= 0) & (n < chunks) & (pos + h < places))
            def _():
                q = pos + h
                wait_block(2 * q + core, n)

                @pl.when(pos > 0)
                def _():
                    forward(q, n, me - 2).start()

                to_sib(q, n).start()

        n = t - (places - 1)

        @pl.when((n >= 0) & (n < chunks))
        def _():
            @pl.when(n + 1 < chunks)
            def _():
                load_mom(n + 1).start()

            load_mom(n).wait()
            for q in range(places):
                wait_block(2 * q + 1 - core, n)
            out_copy(n).start()
            folded = []
            for s in range(width // GROUP):
                at_cols = pl.ds(pl.multiple_of(n * width + s * GROUP, GROUP), GROUP)
                tok = g_all[:, :, at_cols].reshape(n_fsdp * toks, GROUP)
                grad = dot(at_v[...], tok)
                state = mom[lax.rem(n, 2), :, s * GROUP:(s + 1) * GROUP]
                full = momentum_decay * state.astype(jnp.float32) + grad
                both = dot(full.astype(BF16), fold[...])
                half = both.shape[1] // 2
                folded.append(both[:, :half] + both[:, half:])
            part = jnp.concatenate(folded, axis=1)
            high = part.astype(BF16)
            low = (part - high.astype(jnp.float32)).astype(BF16)
            coeff = dot(rh[...], high) + dot(rh[...], low) + dot(rl[...], high)
            c_all[rep, :, low_cols(n)] = (coeff * mask[...]).astype(BF16)
            for d in range(1, n_rep):
                c_copy(d, n).start()

        m = n - LAG

        @pl.when((m >= 0) & (m < chunks))
        def _():
            for d in range(1, n_rep):
                r = lax.rem(rep + d, n_rep)
                piece = c_all.at[r, :, low_cols(m)]
                pltpu.make_async_copy(piece, piece, c_recv.at[r, m]).wait()
            total = c_all[0, :, low_cols(m)].astype(jnp.float32)
            for r in range(1, n_rep):
                total += c_all[r, :, low_cols(m)].astype(jnp.float32)
            mean_out[:, low_cols(m)] = (total * (1.0 / n_rep)).astype(BF16)
            own_out[:, low_cols(m)] = c_all[rep, :, low_cols(m)]

        return 0

    lax.fori_loop(0, chunks + places - 1 + LAG, step, 0)

    at_copy.wait()
    for d in range(1, n_fsdp):
        acts_copy(d).wait_send()

    def drain(n, _):
        out_copy(n).wait()

        @pl.when(pos + 1 < places)
        def _():
            own_right(n).wait_send()

        @pl.when(pos > 0)
        def _():
            own_left(n).wait_send()

        own_sib(n).wait_send()
        for h in range(1, places):
            @pl.when(pos >= h)
            def _():
                @pl.when(pos + 1 < places)
                def _():
                    forward(pos - h, n, me + 2).wait_send()

                to_sib(pos - h, n).wait_send()

            @pl.when(pos + h < places)
            def _():
                @pl.when(pos > 0)
                def _():
                    forward(pos + h, n, me - 2).wait_send()

                to_sib(pos + h, n).wait_send()

        for d in range(1, n_rep):
            c_copy(d, n).wait_send()
        return 0

    lax.fori_loop(0, chunks, drain, 0)


def finish_kernel(at, g, momentum, own, mean, unfold, spread, fresh, update):
    width = momentum.shape[2]
    low = GROUP // BLOCK * LOW

    def spread_rows(c):
        return dot(spread[...], jnp.concatenate([c, c], axis=0)).astype(BF16)

    own_rows = spread_rows(own[...])
    mean_rows = spread_rows(mean[...])
    for s in range(width // GROUP):
        here = slice(s * GROUP, (s + 1) * GROUP)
        lanes = slice(s * low, (s + 1) * low)
        tok = g[:, :, here].reshape(at.shape[1], GROUP)
        full = momentum_decay * momentum[0, :, here].astype(jnp.float32) + dot(at[...], tok)
        piece = own_rows[:, lanes]
        shaped = dot(jnp.concatenate([piece, piece], axis=1), unfold[...])
        fresh[0, :, here] = (full - shaped).astype(BF16)
        piece = mean_rows[:, lanes]
        update[:, here] = dot(jnp.concatenate([piece, piece], axis=1), unfold[...]).astype(BF16)


def shards(n_rep, n_fsdp, acts, grad_out, momentum, band):
    toks, cols = grad_out.shape
    rows = momentum.shape[1]
    width = 1024 if cols % 1024 == 0 else GROUP
    if n_fsdp > 8:
        width = 2048
    chunks = cols // width
    places = n_fsdp // 2
    fold, unfold, rh, rl, spread = [jnp.asarray(t) for t in tables(rows)]
    low_rows = rows // BLOCK * LOW
    low_cols = cols // BLOCK * LOW
    low_width = width // BLOCK * LOW
    tokens = toks * n_fsdp
    vmem = pl.BlockSpec(memory_space=pltpu.VMEM)
    hbm = pl.BlockSpec(memory_space=pl.ANY)
    dma = pltpu.SemaphoreType.DMA
    at, g, own, mean = pl.pallas_call(
        functools.partial(gather_kernel, n_rep, n_fsdp, width, chunks),
        out_shape=(
            jax.ShapeDtypeStruct((rows, tokens), BF16),
            jax.ShapeDtypeStruct((n_fsdp, toks, cols), BF16),
            jax.ShapeDtypeStruct((low_rows, low_cols), BF16),
            jax.ShapeDtypeStruct((low_rows, low_cols), BF16),
        ),
        in_specs=[pl.BlockSpec(memory_space=pltpu.SMEM), hbm, hbm, hbm, vmem, vmem, vmem],
        out_specs=(hbm, hbm, vmem, vmem),
        scratch_shapes=[
            pltpu.VMEM((n_fsdp, toks, rows), BF16),
            pltpu.VMEM((n_fsdp, toks, cols), BF16),
            pltpu.VMEM((rows, tokens), BF16),
            pltpu.VMEM((2, rows, width), BF16),
            pltpu.VMEM((n_rep, low_rows, low_cols), BF16),
            pltpu.VMEM((low_rows, low_width), jnp.float32),
            dma((n_fsdp,)), dma((n_fsdp,)), dma, dma,
            dma((n_fsdp, chunks)), dma((places, chunks)), dma((chunks,)), dma((places, chunks)),
            dma((2,)), dma((n_rep, chunks)), dma((n_rep, chunks)), dma((chunks,)), dma,
        ],
        compiler_params=pltpu.CompilerParams(
            collective_id=0, has_side_effects=True, vmem_limit_bytes=56 * 2**20
        ),
        cost_estimate=pl.CostEstimate(
            flops=4 * rows * tokens * cols, bytes_accessed=2 * rows * cols, transcendentals=0
        ),
        name="gather",
    )(band, acts, grad_out, momentum, fold, rh, rl)
    fresh, update = pl.pallas_call(
        finish_kernel,
        grid=(cols // 1024,),
        out_shape=(
            jax.ShapeDtypeStruct((1, rows, cols), BF16),
            jax.ShapeDtypeStruct((rows, cols), BF16),
        ),
        in_specs=[
            vmem,
            pl.BlockSpec((n_fsdp, toks, 1024), lambda n: (0, 0, n)),
            pl.BlockSpec((1, rows, 1024), lambda n: (0, 0, n)),
            pl.BlockSpec((low_rows, 256), lambda n: (0, n)),
            pl.BlockSpec((low_rows, 256), lambda n: (0, n)),
            vmem,
            vmem,
        ],
        out_specs=(
            pl.BlockSpec((1, rows, 1024), lambda n: (0, 0, n)),
            pl.BlockSpec((rows, 1024), lambda n: (0, n)),
        ),
        compiler_params=pltpu.CompilerParams(vmem_limit_bytes=56 * 2**20),
        cost_estimate=pl.CostEstimate(
            flops=8 * rows * tokens * cols, bytes_accessed=7 * rows * cols, transcendentals=0
        ),
        name="finish",
    )(at, g, momentum, own, mean, unfold, spread)
    return fresh, update


def solution(mesh):
    placed = (P(("rep", "fsdp"), None), P(("rep", "fsdp"), None), P("rep", "fsdp", None), P())
    return jax.shard_map(
        functools.partial(shards, mesh.shape["rep"], mesh.shape["fsdp"]),
        mesh=mesh,
        in_specs=placed,
        out_specs=(P("rep", "fsdp", None), P("fsdp", None)),
        check_vma=False,
    )
```

```python
import functools

import jax
import jax.numpy as jnp
import ml_dtypes
import numpy as np
from jax import lax
from jax.experimental import pallas as pl
from jax.experimental.pallas import tpu as pltpu
from jax.sharding import PartitionSpec as P

BLOCK = 64
LOW = 16
GROUP = 512
LAG = 1

momentum_decay = 0.999
MESH = pl.DeviceIdType.MESH
BF16 = jnp.bfloat16


def dct_low():
    u = np.arange(LOW, dtype=np.float64)[:, None]
    a = np.arange(BLOCK, dtype=np.float64)[None, :]
    scale = np.where(u == 0, np.sqrt(1.0 / BLOCK), np.sqrt(2.0 / BLOCK))
    return scale * np.cos(np.pi * (2 * a + 1) * u / (2 * BLOCK))


def tables(rows):
    low_dct = dct_low()
    all_cols = np.kron(np.eye(GROUP // BLOCK), low_dct)
    all_rows = np.kron(np.eye(rows // BLOCK), low_dct)
    ch, cl = np_split(all_cols)
    rh, rl = np_split(all_rows)
    fold = np.concatenate([ch.T, cl.T], axis=1)
    unfold = np.concatenate([ch, cl], axis=0)
    spread = np.concatenate([rh.T, rl.T], axis=1)
    return fold, unfold, rh, rl, spread


def np_split(table):
    high = table.astype(ml_dtypes.bfloat16)
    low = (table - high.astype(np.float64)).astype(ml_dtypes.bfloat16)
    return high, low


def dot(a, b):
    return jnp.dot(a, b, preferred_element_type=jnp.float32)


def gather_kernel(
    n_rep, n_fsdp, width, chunks,
    band, acts, gout, momentum, fold, rh, rl, unfold, spread,
    fresh_out, mean_out,
    acts_all, g_all, at_v, mom, full_v, c_all, mask,
    a_recv, a_send, a_local, g_local, g_recv, line_send, left_send, sib_send,
    m_sem, c_recv, c_send,
):
    rep = lax.axis_index("rep")
    me = lax.axis_index("fsdp")
    core = lax.rem(me, 2)
    pos = me // 2
    places = n_fsdp // 2
    sib = me + 1 - 2 * core
    rows = at_v.shape[0]
    toks = gout.shape[0]
    low_width = width // BLOCK * LOW

    barrier = pltpu.get_barrier_semaphore()
    for d in range(1, n_fsdp):
        pl.semaphore_signal(
            barrier, inc=1, device_id=(rep, lax.rem(me + d, n_fsdp)), device_id_type=MESH
        )
    for d in range(1, n_rep):
        pl.semaphore_signal(
            barrier, inc=1, device_id=(lax.rem(rep + d, n_rep), me), device_id_type=MESH
        )

    def cols(n):
        return pl.ds(pl.multiple_of(n * width, width), width)

    def low_cols(n):
        return pl.ds(pl.multiple_of(n * low_width, low_width), low_width)

    def load_mom(n):
        return pltpu.make_async_copy(
            momentum.at[0, :, cols(n)], mom.at[lax.rem(n, 2)], m_sem.at[lax.rem(n, 2)]
        )

    own_acts = pltpu.make_async_copy(
        acts.at[:, pl.ds(pl.multiple_of(me * rows, rows), rows)], acts_all.at[me], a_local
    )
    own_acts.start()
    own_g = pltpu.make_async_copy(gout, g_all.at[me], g_local)
    own_g.start()
    load_mom(0).start()

    pl.semaphore_wait(barrier, n_fsdp - 1 + n_rep - 1)

    def acts_copy(d):
        peer = lax.rem(me + d, n_fsdp)
        return pltpu.make_async_remote_copy(
            src_ref=acts.at[:, pl.ds(pl.multiple_of(peer * rows, rows), rows)],
            dst_ref=acts_all.at[me],
            send_sem=a_send.at[d],
            recv_sem=a_recv.at[me],
            device_id=(rep, peer),
            device_id_type=MESH,
        )

    def g_copy(src, b, n, send, target):
        return pltpu.make_async_remote_copy(
            src_ref=src,
            dst_ref=g_all.at[b, :, cols(n)],
            send_sem=send,
            recv_sem=g_recv.at[b, n],
            device_id=(rep, target),
            device_id_type=MESH,
        )

    def slot(b, n):
        return g_all.at[b, :, cols(n)]

    def own_right(n):
        return g_copy(gout.at[:, cols(n)], me, n, line_send.at[pos, n], me + 2)

    def own_left(n):
        return g_copy(gout.at[:, cols(n)], me, n, left_send.at[n], me - 2)

    def own_sib(n):
        return g_copy(gout.at[:, cols(n)], me, n, sib_send.at[pos, n], sib)

    def forward(q, n, target):
        b = 2 * q + core
        return g_copy(slot(b, n), b, n, line_send.at[q, n], target)

    def to_sib(q, n):
        b = 2 * q + core
        return g_copy(slot(b, n), b, n, sib_send.at[q, n], sib)

    def wait_block(b, n):
        pltpu.make_async_copy(slot(b, n), slot(b, n), g_recv.at[b, n]).wait()

    def send_own(n):
        @pl.when(pos + 1 < places)
        def _():
            own_right(n).start()

        @pl.when(pos > 0)
        def _():
            own_left(n).start()

        own_sib(n).start()

    def c_copy(d, n):
        peer = lax.rem(rep + d, n_rep)
        return pltpu.make_async_remote_copy(
            src_ref=c_all.at[rep, :, low_cols(n)],
            dst_ref=c_all.at[rep, :, low_cols(n)],
            send_sem=c_send.at[d, n],
            recv_sem=c_recv.at[rep, n],
            device_id=(peer, me),
            device_id_type=MESH,
        )

    for d in range(1, n_fsdp):
        acts_copy(d).start()
    send_own(0)
    send_own(1)

    low_rows = lax.broadcasted_iota(jnp.int32, mask.shape, 0)
    low_lanes = lax.broadcasted_iota(jnp.int32, mask.shape, 1)
    place = lax.rem(low_rows, LOW) * BLOCK + lax.rem(low_lanes, LOW)
    kept = jnp.zeros(mask.shape, jnp.float32)
    for k in range(band.shape[0]):
        kept = jnp.where(place == band[k], 1.0, kept)
    mask[...] = kept

    own_acts.wait()
    own_g.wait()
    for d in range(1, n_fsdp):
        b = lax.rem(me + d, n_fsdp)
        pltpu.make_async_copy(acts_all.at[b], acts_all.at[b], a_recv.at[b]).wait()
    for b in range(n_fsdp):
        at_v[:, b * toks:(b + 1) * toks] = (
            acts_all[b].astype(jnp.float32).T.astype(BF16)
        )

    def step(t, _):
        @pl.when(t + 2 < chunks)
        def _():
            send_own(t + 2)

        for h in range(1, places):
            n = t + 1 - h

            @pl.when((n >= 0) & (n < chunks) & (pos >= h))
            def _():
                q = pos - h
                wait_block(2 * q + core, n)

                @pl.when(pos + 1 < places)
                def _():
                    forward(q, n, me + 2).start()

                to_sib(q, n).start()

            @pl.when((n >= 0) & (n < chunks) & (pos + h < places))
            def _():
                q = pos + h
                wait_block(2 * q + core, n)

                @pl.when(pos > 0)
                def _():
                    forward(q, n, me - 2).start()

                to_sib(q, n).start()

        n = t - (places - 1)

        @pl.when((n >= 0) & (n < chunks))
        def _():
            @pl.when(n + 1 < chunks)
            def _():
                load_mom(n + 1).start()

            load_mom(n).wait()
            for q in range(places):
                wait_block(2 * q + 1 - core, n)
            folded = []
            for s in range(width // GROUP):
                at_cols = pl.ds(pl.multiple_of(n * width + s * GROUP, GROUP), GROUP)
                tok = g_all[:, :, at_cols].reshape(n_fsdp * toks, GROUP)
                grad = dot(at_v[...], tok)
                state = mom[lax.rem(n, 2), :, s * GROUP:(s + 1) * GROUP]
                full = momentum_decay * state.astype(jnp.float32) + grad
                full_v[:, s * GROUP:(s + 1) * GROUP] = full
                both = dot(full.astype(BF16), fold[...])
                half = both.shape[1] // 2
                folded.append(both[:, :half] + both[:, half:])
            part = jnp.concatenate(folded, axis=1)
            high = part.astype(BF16)
            low = (part - high.astype(jnp.float32)).astype(BF16)
            coeff = dot(rh[...], high) + dot(rh[...], low) + dot(rl[...], high)
            own = (coeff * mask[...]).astype(BF16)
            c_all[rep, :, low_cols(n)] = own
            for d in range(1, n_rep):
                c_copy(d, n).start()

            own_rows = dot(spread[...], jnp.concatenate([own, own], axis=0)).astype(BF16)
            low = GROUP // BLOCK * LOW
            for s in range(width // GROUP):
                here = slice(s * GROUP, (s + 1) * GROUP)
                there = pl.ds(pl.multiple_of(n * width + s * GROUP, GROUP), GROUP)
                piece = own_rows[:, s * low:(s + 1) * low]
                shaped = dot(jnp.concatenate([piece, piece], axis=1), unfold[...])
                fresh_out[:, there] = (full_v[:, here] - shaped).astype(BF16)

        m = n - LAG

        @pl.when((m >= 0) & (m < chunks))
        def _():
            for d in range(1, n_rep):
                r = lax.rem(rep + d, n_rep)
                piece = c_all.at[r, :, low_cols(m)]
                pltpu.make_async_copy(piece, piece, c_recv.at[r, m]).wait()
            total = c_all[0, :, low_cols(m)].astype(jnp.float32)
            for r in range(1, n_rep):
                total += c_all[r, :, low_cols(m)].astype(jnp.float32)
            mean_out[:, low_cols(m)] = (total * (1.0 / n_rep)).astype(BF16)

        return 0

    lax.fori_loop(0, chunks + places - 1 + LAG, step, 0)

    for d in range(1, n_fsdp):
        acts_copy(d).wait_send()

    def drain(n, _):
        @pl.when(pos + 1 < places)
        def _():
            own_right(n).wait_send()

        @pl.when(pos > 0)
        def _():
            own_left(n).wait_send()

        own_sib(n).wait_send()
        for h in range(1, places):
            @pl.when(pos >= h)
            def _():
                @pl.when(pos + 1 < places)
                def _():
                    forward(pos - h, n, me + 2).wait_send()

                to_sib(pos - h, n).wait_send()

            @pl.when(pos + h < places)
            def _():
                @pl.when(pos > 0)
                def _():
                    forward(pos + h, n, me - 2).wait_send()

                to_sib(pos + h, n).wait_send()

        for d in range(1, n_rep):
            c_copy(d, n).wait_send()
        return 0

    lax.fori_loop(0, chunks, drain, 0)


def finish_kernel(fresh_in, mean, unfold, spread, fresh, update, sem):
    width = update.shape[1]
    low = GROUP // BLOCK * LOW
    n = pl.program_id(0)

    def copy(n):
        here = pl.ds(pl.multiple_of(n * width, width), width)
        return pltpu.make_async_copy(fresh_in.at[:, here], fresh.at[0, :, here], sem.at[n])

    copy(n).start()
    coeff = mean[:, pl.ds(pl.multiple_of(n * (width // BLOCK * LOW), 128), width // BLOCK * LOW)]
    mean_rows = dot(spread[...], jnp.concatenate([coeff, coeff], axis=0)).astype(BF16)
    for s in range(width // GROUP):
        piece = mean_rows[:, s * low:(s + 1) * low]
        update[:, s * GROUP:(s + 1) * GROUP] = dot(
            jnp.concatenate([piece, piece], axis=1), unfold[...]
        ).astype(BF16)

    @pl.when(n == sem.shape[0] - 1)
    def _():
        for k in range(sem.shape[0]):
            copy(k).wait()


def shards(n_rep, n_fsdp, acts, grad_out, momentum, band):
    toks, cols = grad_out.shape
    rows = momentum.shape[1]
    width = 1024 if cols % 1024 == 0 else GROUP
    if n_fsdp > 8:
        width = 2048
    chunks = cols // width
    places = n_fsdp // 2
    fold, unfold, rh, rl, spread = [jnp.asarray(t) for t in tables(rows)]
    low_rows = rows // BLOCK * LOW
    low_cols = cols // BLOCK * LOW
    low_width = width // BLOCK * LOW
    tokens = toks * n_fsdp
    vmem = pl.BlockSpec(memory_space=pltpu.VMEM)
    hbm = pl.BlockSpec(memory_space=pl.ANY)
    dma = pltpu.SemaphoreType.DMA
    fresh_in, mean = pl.pallas_call(
        functools.partial(gather_kernel, n_rep, n_fsdp, width, chunks),
        out_shape=(
            pltpu.VMEM((rows, cols), BF16),
            pltpu.VMEM((low_rows, low_cols), BF16),
        ),
        in_specs=[pl.BlockSpec(memory_space=pltpu.SMEM), hbm, hbm, hbm] + [vmem] * 5,
        out_specs=(vmem, vmem),
        scratch_shapes=[
            pltpu.VMEM((n_fsdp, toks, rows), BF16),
            pltpu.VMEM((n_fsdp, toks, cols), BF16),
            pltpu.VMEM((rows, tokens), BF16),
            pltpu.VMEM((2, rows, width), BF16),
            pltpu.VMEM((rows, width), jnp.float32),
            pltpu.VMEM((n_rep, low_rows, low_cols), BF16),
            pltpu.VMEM((low_rows, low_width), jnp.float32),
            dma((n_fsdp,)), dma((n_fsdp,)), dma, dma,
            dma((n_fsdp, chunks)), dma((places, chunks)), dma((chunks,)), dma((places, chunks)),
            dma((2,)), dma((n_rep, chunks)), dma((n_rep, chunks)),
        ],
        compiler_params=pltpu.CompilerParams(
            collective_id=0, has_side_effects=True, vmem_limit_bytes=44 * 2**20
        ),
        cost_estimate=pl.CostEstimate(
            flops=4 * rows * tokens * cols, bytes_accessed=2 * rows * cols, transcendentals=0
        ),
        name="gather",
    )(band, acts, grad_out, momentum, fold, rh, rl, unfold, spread)
    fresh, update = pl.pallas_call(
        finish_kernel,
        grid=(cols // 1024,),
        out_shape=(
            jax.ShapeDtypeStruct((1, rows, cols), BF16),
            jax.ShapeDtypeStruct((rows, cols), BF16),
        ),
        in_specs=[
            vmem,
            vmem,
            vmem,
            vmem,
        ],
        out_specs=(
            hbm,
            pl.BlockSpec((rows, 1024), lambda n: (0, n)),
        ),
        scratch_shapes=[dma((cols // 1024,))],
        compiler_params=pltpu.CompilerParams(vmem_limit_bytes=24 * 2**20),
        cost_estimate=pl.CostEstimate(
            flops=8 * rows * tokens * cols, bytes_accessed=7 * rows * cols, transcendentals=0
        ),
        name="finish",
    )(fresh_in, mean, unfold, spread)
    return fresh, update


def solution(mesh):
    placed = (P(("rep", "fsdp"), None), P(("rep", "fsdp"), None), P("rep", "fsdp", None), P())
    return jax.shard_map(
        functools.partial(shards, mesh.shape["rep"], mesh.shape["fsdp"]),
        mesh=mesh,
        in_specs=placed,
        out_specs=(P("rep", "fsdp", None), P("fsdp", None)),
        check_vma=False,
    )
```

```python
import functools

import jax
import jax.numpy as jnp
import ml_dtypes
import numpy as np
from jax import lax
from jax.experimental import pallas as pl
from jax.experimental.pallas import tpu as pltpu
from jax.sharding import PartitionSpec as P

BLOCK = 64
LOW = 16
GROUP = 512
LAG = 1

momentum_decay = 0.999
MESH = pl.DeviceIdType.MESH
BF16 = jnp.bfloat16


def dct_low():
    u = np.arange(LOW, dtype=np.float64)[:, None]
    a = np.arange(BLOCK, dtype=np.float64)[None, :]
    scale = np.where(u == 0, np.sqrt(1.0 / BLOCK), np.sqrt(2.0 / BLOCK))
    return scale * np.cos(np.pi * (2 * a + 1) * u / (2 * BLOCK))


def tables(rows):
    low_dct = dct_low()
    all_cols = np.kron(np.eye(GROUP // BLOCK), low_dct)
    all_rows = np.kron(np.eye(rows // BLOCK), low_dct)
    ch, cl = np_split(all_cols)
    rh, rl = np_split(all_rows)
    fold = np.concatenate([ch.T, cl.T], axis=1)
    unfold = np.concatenate([ch, cl], axis=0)
    spread = np.concatenate([rh.T, rl.T], axis=1)
    return fold, unfold, rh, rl, spread


def np_split(table):
    high = table.astype(ml_dtypes.bfloat16)
    low = (table - high.astype(np.float64)).astype(ml_dtypes.bfloat16)
    return high, low


def dot(a, b):
    return jnp.dot(a, b, preferred_element_type=jnp.float32)


def gather_kernel(
    n_rep, n_fsdp, width, chunks,
    band, acts, gout, momentum, fold, rh, rl, unfold, spread,
    fresh_out, mean_out,
    acts_all, g_all, at_v, mom, full_v, c_all, mask,
    a_recv, a_send, a_local, g_local, g_recv, line_send, left_send, sib_send,
    m_sem, c_recv, c_send,
):
    rep = lax.axis_index("rep")
    me = lax.axis_index("fsdp")
    core = lax.rem(me, 2)
    pos = me // 2
    places = n_fsdp // 2
    sib = me + 1 - 2 * core
    rows = at_v.shape[0]
    toks = gout.shape[0]
    low_width = width // BLOCK * LOW

    barrier = pltpu.get_barrier_semaphore()
    for d in range(1, n_fsdp):
        pl.semaphore_signal(
            barrier, inc=1, device_id=(rep, lax.rem(me + d, n_fsdp)), device_id_type=MESH
        )
    for d in range(1, n_rep):
        pl.semaphore_signal(
            barrier, inc=1, device_id=(lax.rem(rep + d, n_rep), me), device_id_type=MESH
        )

    def cols(n):
        return pl.ds(pl.multiple_of(n * width, width), width)

    def low_cols(n):
        return pl.ds(pl.multiple_of(n * low_width, low_width), low_width)

    def load_mom(n):
        return pltpu.make_async_copy(
            momentum.at[0, :, cols(n)], mom.at[lax.rem(n, 2)], m_sem.at[lax.rem(n, 2)]
        )

    own_acts = pltpu.make_async_copy(
        acts.at[:, pl.ds(pl.multiple_of(me * rows, rows), rows)], acts_all.at[me], a_local
    )
    own_acts.start()
    own_g = pltpu.make_async_copy(gout, g_all.at[me], g_local)
    own_g.start()
    load_mom(0).start()

    pl.semaphore_wait(barrier, n_fsdp - 1 + n_rep - 1)

    def acts_copy(d):
        peer = lax.rem(me + d, n_fsdp)
        return pltpu.make_async_remote_copy(
            src_ref=acts.at[:, pl.ds(pl.multiple_of(peer * rows, rows), rows)],
            dst_ref=acts_all.at[me],
            send_sem=a_send.at[d],
            recv_sem=a_recv.at[me],
            device_id=(rep, peer),
            device_id_type=MESH,
        )

    def g_copy(src, b, n, send, target):
        return pltpu.make_async_remote_copy(
            src_ref=src,
            dst_ref=g_all.at[b, :, cols(n)],
            send_sem=send,
            recv_sem=g_recv.at[b, n],
            device_id=(rep, target),
            device_id_type=MESH,
        )

    def slot(b, n):
        return g_all.at[b, :, cols(n)]

    def own_right(n):
        return g_copy(gout.at[:, cols(n)], me, n, line_send.at[pos, n], me + 2)

    def own_left(n):
        return g_copy(gout.at[:, cols(n)], me, n, left_send.at[n], me - 2)

    def own_sib(n):
        return g_copy(gout.at[:, cols(n)], me, n, sib_send.at[pos, n], sib)

    def forward(q, n, target):
        b = 2 * q + core
        return g_copy(slot(b, n), b, n, line_send.at[q, n], target)

    def to_sib(q, n):
        b = 2 * q + core
        return g_copy(slot(b, n), b, n, sib_send.at[q, n], sib)

    def wait_block(b, n):
        pltpu.make_async_copy(slot(b, n), slot(b, n), g_recv.at[b, n]).wait()

    def send_own(n):
        @pl.when(pos + 1 < places)
        def _():
            own_right(n).start()

        @pl.when(pos > 0)
        def _():
            own_left(n).start()

        own_sib(n).start()

    def c_copy(d, n):
        peer = lax.rem(rep + d, n_rep)
        return pltpu.make_async_remote_copy(
            src_ref=c_all.at[rep, :, low_cols(n)],
            dst_ref=c_all.at[rep, :, low_cols(n)],
            send_sem=c_send.at[d, n],
            recv_sem=c_recv.at[rep, n],
            device_id=(peer, me),
            device_id_type=MESH,
        )

    for d in range(1, n_fsdp):
        acts_copy(d).start()
    send_own(0)
    send_own(1)

    low_rows = lax.broadcasted_iota(jnp.int32, mask.shape, 0)
    low_lanes = lax.broadcasted_iota(jnp.int32, mask.shape, 1)
    place = lax.rem(low_rows, LOW) * BLOCK + lax.rem(low_lanes, LOW)
    kept = jnp.zeros(mask.shape, jnp.float32)
    for k in range(band.shape[0]):
        kept = jnp.where(place == band[k], 1.0, kept)
    mask[...] = kept

    own_acts.wait()
    own_g.wait()
    for d in range(1, n_fsdp):
        b = lax.rem(me + d, n_fsdp)
        pltpu.make_async_copy(acts_all.at[b], acts_all.at[b], a_recv.at[b]).wait()
    for b in range(n_fsdp):
        at_v[:, b * toks:(b + 1) * toks] = (
            acts_all[b].astype(jnp.float32).T.astype(BF16)
        )

    def step(t, _):
        @pl.when(t + 2 < chunks)
        def _():
            send_own(t + 2)

        for h in range(1, places):
            n = t + 1 - h

            @pl.when((n >= 0) & (n < chunks) & (pos >= h))
            def _():
                q = pos - h
                wait_block(2 * q + core, n)

                @pl.when(pos + 1 < places)
                def _():
                    forward(q, n, me + 2).start()

                to_sib(q, n).start()

            @pl.when((n >= 0) & (n < chunks) & (pos + h < places))
            def _():
                q = pos + h
                wait_block(2 * q + core, n)

                @pl.when(pos > 0)
                def _():
                    forward(q, n, me - 2).start()

                to_sib(q, n).start()

        n = t - (places - 1)

        @pl.when((n >= 0) & (n < chunks))
        def _():
            @pl.when(n + 1 < chunks)
            def _():
                load_mom(n + 1).start()

            load_mom(n).wait()
            for q in range(places):
                wait_block(2 * q + 1 - core, n)
            folded = []
            for s in range(width // GROUP):
                at_cols = pl.ds(pl.multiple_of(n * width + s * GROUP, GROUP), GROUP)
                tok = g_all[:, :, at_cols].reshape(n_fsdp * toks, GROUP)
                grad = dot(at_v[...], tok)
                state = mom[lax.rem(n, 2), :, s * GROUP:(s + 1) * GROUP]
                full = momentum_decay * state.astype(jnp.float32) + grad
                full_v[:, s * GROUP:(s + 1) * GROUP] = full
                both = dot(full.astype(BF16), fold[...])
                half = both.shape[1] // 2
                folded.append(both[:, :half] + both[:, half:])
            part = jnp.concatenate(folded, axis=1)
            high = part.astype(BF16)
            low = (part - high.astype(jnp.float32)).astype(BF16)
            coeff = dot(rh[...], high) + dot(rh[...], low) + dot(rl[...], high)
            own = (coeff * mask[...]).astype(BF16)
            c_all[rep, :, low_cols(n)] = own
            for d in range(1, n_rep):
                c_copy(d, n).start()

            own_rows = dot(spread[...], jnp.concatenate([own, own], axis=0)).astype(BF16)
            low = GROUP // BLOCK * LOW
            for s in range(width // GROUP):
                here = slice(s * GROUP, (s + 1) * GROUP)
                there = pl.ds(pl.multiple_of(n * width + s * GROUP, GROUP), GROUP)
                piece = own_rows[:, s * low:(s + 1) * low]
                shaped = dot(jnp.concatenate([piece, piece], axis=1), unfold[...])
                fresh_out[:, there] = (full_v[:, here] - shaped).astype(BF16)

        m = n - LAG

        @pl.when((m >= 0) & (m < chunks))
        def _():
            for d in range(1, n_rep):
                r = lax.rem(rep + d, n_rep)
                piece = c_all.at[r, :, low_cols(m)]
                pltpu.make_async_copy(piece, piece, c_recv.at[r, m]).wait()
            total = c_all[0, :, low_cols(m)].astype(jnp.float32)
            for r in range(1, n_rep):
                total += c_all[r, :, low_cols(m)].astype(jnp.float32)
            mean_out[:, low_cols(m)] = (total * (1.0 / n_rep)).astype(BF16)

        return 0

    lax.fori_loop(0, chunks + places - 1 + LAG, step, 0)

    for d in range(1, n_fsdp):
        acts_copy(d).wait_send()

    def drain(n, _):
        @pl.when(pos + 1 < places)
        def _():
            own_right(n).wait_send()

        @pl.when(pos > 0)
        def _():
            own_left(n).wait_send()

        own_sib(n).wait_send()
        for h in range(1, places):
            @pl.when(pos >= h)
            def _():
                @pl.when(pos + 1 < places)
                def _():
                    forward(pos - h, n, me + 2).wait_send()

                to_sib(pos - h, n).wait_send()

            @pl.when(pos + h < places)
            def _():
                @pl.when(pos > 0)
                def _():
                    forward(pos + h, n, me - 2).wait_send()

                to_sib(pos + h, n).wait_send()

        for d in range(1, n_rep):
            c_copy(d, n).wait_send()
        return 0

    lax.fori_loop(0, chunks, drain, 0)


def finish_kernel(fresh_in, mean, unfold, spread, fresh, update, sem):
    width = update.shape[1]
    low = GROUP // BLOCK * LOW
    n = pl.program_id(0)

    def copy(n):
        here = pl.ds(pl.multiple_of(n * width, width), width)
        return pltpu.make_async_copy(fresh_in.at[:, here], fresh.at[0, :, here], sem.at[n])

    @pl.when(n == 0)
    def _():
        for k in range(sem.shape[0]):
            copy(k).start()

    coeff = mean[:, pl.ds(pl.multiple_of(n * (width // BLOCK * LOW), 128), width // BLOCK * LOW)]
    mean_rows = dot(spread[...], jnp.concatenate([coeff, coeff], axis=0)).astype(BF16)
    for s in range(width // GROUP):
        piece = mean_rows[:, s * low:(s + 1) * low]
        update[:, s * GROUP:(s + 1) * GROUP] = dot(
            jnp.concatenate([piece, piece], axis=1), unfold[...]
        ).astype(BF16)

    @pl.when(n == sem.shape[0] - 1)
    def _():
        for k in range(sem.shape[0]):
            copy(k).wait()


def shards(n_rep, n_fsdp, acts, grad_out, momentum, band):
    toks, cols = grad_out.shape
    rows = momentum.shape[1]
    width = 1024 if cols % 1024 == 0 else GROUP
    if n_fsdp > 8:
        width = 2048
    chunks = cols // width
    places = n_fsdp // 2
    fold, unfold, rh, rl, spread = [jnp.asarray(t) for t in tables(rows)]
    low_rows = rows // BLOCK * LOW
    low_cols = cols // BLOCK * LOW
    low_width = width // BLOCK * LOW
    tokens = toks * n_fsdp
    vmem = pl.BlockSpec(memory_space=pltpu.VMEM)
    hbm = pl.BlockSpec(memory_space=pl.ANY)
    dma = pltpu.SemaphoreType.DMA
    fresh_in, mean = pl.pallas_call(
        functools.partial(gather_kernel, n_rep, n_fsdp, width, chunks),
        out_shape=(
            pltpu.VMEM((rows, cols), BF16),
            pltpu.VMEM((low_rows, low_cols), BF16),
        ),
        in_specs=[pl.BlockSpec(memory_space=pltpu.SMEM), hbm, hbm, hbm] + [vmem] * 5,
        out_specs=(vmem, vmem),
        scratch_shapes=[
            pltpu.VMEM((n_fsdp, toks, rows), BF16),
            pltpu.VMEM((n_fsdp, toks, cols), BF16),
            pltpu.VMEM((rows, tokens), BF16),
            pltpu.VMEM((2, rows, width), BF16),
            pltpu.VMEM((rows, width), jnp.float32),
            pltpu.VMEM((n_rep, low_rows, low_cols), BF16),
            pltpu.VMEM((low_rows, low_width), jnp.float32),
            dma((n_fsdp,)), dma((n_fsdp,)), dma, dma,
            dma((n_fsdp, chunks)), dma((places, chunks)), dma((chunks,)), dma((places, chunks)),
            dma((2,)), dma((n_rep, chunks)), dma((n_rep, chunks)),
        ],
        compiler_params=pltpu.CompilerParams(
            collective_id=0, has_side_effects=True, vmem_limit_bytes=44 * 2**20
        ),
        cost_estimate=pl.CostEstimate(
            flops=4 * rows * tokens * cols, bytes_accessed=2 * rows * cols, transcendentals=0
        ),
        name="gather",
    )(band, acts, grad_out, momentum, fold, rh, rl, unfold, spread)
    fresh, update = pl.pallas_call(
        finish_kernel,
        grid=(cols // 1024,),
        out_shape=(
            jax.ShapeDtypeStruct((1, rows, cols), BF16),
            jax.ShapeDtypeStruct((rows, cols), BF16),
        ),
        in_specs=[
            vmem,
            vmem,
            vmem,
            vmem,
        ],
        out_specs=(
            hbm,
            pl.BlockSpec((rows, 1024), lambda n: (0, n)),
        ),
        scratch_shapes=[dma((cols // 1024,))],
        compiler_params=pltpu.CompilerParams(vmem_limit_bytes=24 * 2**20),
        cost_estimate=pl.CostEstimate(
            flops=8 * rows * tokens * cols, bytes_accessed=7 * rows * cols, transcendentals=0
        ),
        name="finish",
    )(fresh_in, mean, unfold, spread)
    return fresh, update


def solution(mesh):
    placed = (P(("rep", "fsdp"), None), P(("rep", "fsdp"), None), P("rep", "fsdp", None), P())
    return jax.shard_map(
        functools.partial(shards, mesh.shape["rep"], mesh.shape["fsdp"]),
        mesh=mesh,
        in_specs=placed,
        out_specs=(P("rep", "fsdp", None), P("fsdp", None)),
        check_vma=False,
    )
```
